512 devices in a mesh: mem: 8 (over y, core), grid: 64 (over x, z).
Axes of the slice: x: 4, y: 4, z: 16, core: 2. Of those that a mesh axis runs over, the one named last changes fastest.
Arguments:
- ensemble: bfloat16 [80, 160, 16384], P('mem', None, 'grid'), may hold values from -6 to 6
- obs_prior: bfloat16 [80, 1048576], P(None, ('mem', 'grid')), may hold values from -15 to 15
- obs_value: bfloat16 [1048576], P(('mem', 'grid')), may hold values from -8 to 8
- obs_precision: bfloat16 [1048576], P(('mem', 'grid')), may hold values from 0.049804688 to 1
- entry_ids: int32 [8, 64, 2, 512], P('mem', 'grid'), may hold values from 0 to 131071, as said below
- entry_count: int32 [8, 64, 2], P('mem', 'grid'), may hold values from 1 to 512, as said below
- entry_taper: float32 [8, 64, 2, 512], P('mem', 'grid'), may hold values from 0.05 to 1
Outputs:
- analysis: bfloat16 [80, 160, 16384], P('mem', None, 'grid')
The draws below stay inside these ranges and needn't reach their ends.
Inputs may be any that keep to these rules, and one draw needn't show every extreme that they name: `entry_ids`: on the devices of mem index m and grid index g, an entry id names observation m * 64 * 2048 + id, held by grid index id // 2048 at row id % 2048. That grid index is g or lies within 4 grid indices of g, counted cyclically. Among one device's 2 * 512 entries at most 128 name any one grid index other than g, and on every device some grid index is named exactly 128 times. `entry_count`: some list is full.
All inputs are finite; a program needn't handle non-finite values.
Results may differ from the reference program's by a relative error of at most 0.0057.
Values may be sent and summed in bfloat16 or wider, within the bound.
A program may use at most 64 MiB of HBM per device.

```python
import math
import jax
import jax.numpy as jnp
from jax import lax

K = 80
BLOCK = 128
C_DEV = 256
MLOC = 512
OBS_DEV = 2048
REACH = 4
CAP = 128
ITERS = 5
V = 160
NB_DEV = 2
NCOL = 16384
NOBS = 1048576
N_MEM = 8
N_GRID = 64


def draw_obs_prior(key, part):
    key = jax.random.fold_in(key, 21)
    first_key, scale_key = jax.random.split(key, 2)
    spread = jnp.exp(jax.random.uniform(scale_key, (1, NOBS), minval=jnp.log(0.3), maxval=jnp.log(3.0)))
    values = jax.random.normal(first_key, (K, NOBS)) * spread
    return jnp.clip(values, -15.0, 15.0).astype(jnp.bfloat16)


def draw_entry_ids(key, part):
    key = jax.random.fold_in(key, 11)
    entries = NB_DEV * MLOC
    neighbours = 2 * REACH
    signed = jnp.concatenate([-jnp.arange(1, REACH + 1, dtype=jnp.int32), jnp.arange(1, REACH + 1, dtype=jnp.int32)])

    def one_device(device_key, flat_index):
        subkeys = jax.random.split(device_key, 4)
        holder_loads = jax.random.randint(subkeys[0], (neighbours,), 0, CAP + 1)
        forced = jax.random.randint(subkeys[1], (), 0, neighbours)
        holder_loads = jnp.where(jnp.arange(neighbours, dtype=jnp.int32) == forced, CAP, holder_loads)
        bounds = jnp.cumsum(holder_loads)
        positions = jnp.arange(entries, dtype=jnp.int32)
        bucket = jnp.sum((positions[:, None] >= bounds[None, :]).astype(jnp.int32), axis=1)
        offset = jnp.where(bucket < neighbours, signed[jnp.minimum(bucket, neighbours - 1)], 0)
        offset = jax.random.permutation(subkeys[2], offset)
        holder = (flat_index % N_GRID + offset) % N_GRID
        row_index = jax.random.randint(subkeys[3], (entries,), 0, OBS_DEV)
        return (holder * OBS_DEV + row_index).reshape(NB_DEV, MLOC)
    device_keys = jax.random.split(key, N_MEM * N_GRID)
    flat_index = jnp.arange(N_MEM * N_GRID, dtype=jnp.int32)
    return jax.vmap(one_device)(device_keys, flat_index).reshape(N_MEM, N_GRID, NB_DEV, MLOC).astype(jnp.int32)


def draw_entry_count(key, part):
    key = jax.random.fold_in(key, 12)
    first_key, second = jax.random.split(key)
    total = N_MEM * N_GRID * NB_DEV
    counts = jax.random.randint(first_key, (total,), 1, MLOC + 1)
    chosen = jax.random.randint(second, (), 0, total)
    counts = jnp.where(jnp.arange(total, dtype=jnp.int32) == chosen, MLOC, counts)
    return counts.reshape(N_MEM, N_GRID, NB_DEV).astype(jnp.int32)


def block_scale(own_key, dims, cuts, low, high):
    def one(dim, parts):
        heights = jax.random.uniform(jax.random.fold_in(jax.random.fold_in(own_key, 6), dim), (parts,), jnp.float32, low / len(cuts), high / len(cuts))
        return jnp.repeat(jnp.exp(heights), dims[dim] // parts).reshape((-1,) + (1,) * (len(dims) - dim - 1))

    gain = one(*cuts[0])
    for cut in cuts[1:]:
        gain = gain * one(*cut)
    return gain


def noise(rng, extent, scale, bound, cuts=(), kind=jnp.bfloat16):
    array = scale * jax.random.normal(rng, extent, jnp.float32)
    if cuts:
        array = array * block_scale(rng, extent, cuts, -0.22, 0.18)
    return jnp.clip(array, -bound, bound).astype(kind)


def setup_inputs(seed: int = 0) -> dict:
    key_of = jax.random.split(jax.random.key(seed), 8)
    ensemble = noise(key_of[0], (K, V, NCOL), 1.0, 6.0, ((0, 8), (2, 64)))
    obs_prior = draw_obs_prior(jax.random.fold_in(key_of[7], 71), 0)
    obs_value = noise(key_of[2], (NOBS,), 1.5, 8.0, ((0, 512),))
    obs_precision = jnp.clip(jnp.exp(math.log(1.0) - 2.9996462 * jax.random.uniform(key_of[3], (NOBS,), jnp.float32) ** block_scale(key_of[3], (NOBS,), ((0, 512),), -0.2, 0.2)), 0.049804688, 1.0).astype(jnp.bfloat16)
    entry_ids = draw_entry_ids(jax.random.fold_in(key_of[7], 71), 0)
    entry_count = draw_entry_count(jax.random.fold_in(key_of[7], 71), 0)
    entry_taper = jnp.clip(jnp.exp(math.log(1.0) - 2.9957323 * jax.random.uniform(key_of[6], (N_MEM, N_GRID, NB_DEV, MLOC), jnp.float32) ** block_scale(key_of[6], (N_MEM, N_GRID, NB_DEV, MLOC), ((0, 8), (1, 64)), -0.2, 0.2)), 0.05, 1.0)
    return dict(ensemble=ensemble, obs_prior=obs_prior, obs_value=obs_value, obs_precision=obs_precision, entry_ids=entry_ids, entry_count=entry_count, entry_taper=entry_taper)


highest = lax.Precision.HIGHEST

def block_transform(gram, drive):
    members = gram.shape[-1]
    identity = jnp.eye(members, dtype=jnp.float32)
    system = gram + (members - 1.0) * identity
    scale = jnp.sqrt(lax.optimization_barrier(jnp.sum(system * system, axis=(1, 2))))
    root_iter = system / scale[:, None, None]
    inverse_root = jnp.broadcast_to(identity, system.shape)
    for sweep_index in range(ITERS):
        update = 1.5 * identity - 0.5 * jnp.einsum('bij,bjk->bik', inverse_root, root_iter, precision=highest)
        root_iter = jnp.einsum('bij,bjk->bik', root_iter, update, precision=highest)
        inverse_root = jnp.einsum('bij,bjk->bik', update, inverse_root, precision=highest)
    spread = jnp.sqrt((members - 1.0) / scale)[:, None, None] * inverse_root
    inner_step = jnp.einsum('bij,bj->bi', inverse_root, drive, precision=highest)
    mean_shift = jnp.einsum('bij,bj->bi', inverse_root, inner_step, precision=highest) / scale[:, None]
    return spread + mean_shift[:, :, None]

def reference(ensemble, obs_prior, obs_value, obs_precision, entry_ids, entry_count, entry_taper):
    base_offset = (jnp.arange(N_MEM, dtype=jnp.int32) * (N_GRID * OBS_DEV))[:, None, None]

    def one_column_group(grid_index):
        listed = lax.dynamic_index_in_dim(entry_ids, grid_index, 1, keepdims=False)
        counted = lax.dynamic_index_in_dim(entry_count, grid_index, 1, keepdims=False)
        tapered = lax.dynamic_index_in_dim(entry_taper, grid_index, 1, keepdims=False)
        absolute = (listed + base_offset).reshape(-1).astype(jnp.int32)
        columns = jnp.take(obs_prior, absolute, axis=1).astype(jnp.float32)
        center = lax.optimization_barrier(jnp.mean(columns, axis=0))
        deviation = columns - center
        innovation = jnp.take(obs_value, absolute).astype(jnp.float32) - center
        precision_taken = jnp.take(obs_precision, absolute).astype(jnp.float32)
        valid_mask = (jnp.arange(MLOC, dtype=jnp.int32)[None, None, :] < counted[:, :, None]).reshape(-1)
        weights = jnp.where(valid_mask, tapered.reshape(-1) * precision_taken, 0.0)
        shaped = deviation.reshape(K, N_MEM, NB_DEV, MLOC)
        weighted = (deviation * weights).reshape(K, N_MEM, NB_DEV, MLOC)
        gram = jnp.einsum('kmbj,lmbj->bkl', weighted, shaped, precision=highest)
        driven = (weights * innovation).reshape(N_MEM, NB_DEV, MLOC)
        drive = jnp.einsum('kmbj,mbj->bk', shaped, driven, precision=highest)
        transform = block_transform(gram, drive).astype(jnp.bfloat16)
        states = lax.dynamic_slice_in_dim(ensemble, grid_index * C_DEV, C_DEV, 2).astype(jnp.float32)
        states = states.reshape(K, V, NB_DEV, BLOCK)
        center_states = lax.optimization_barrier(jnp.mean(states, axis=0))
        anomalies = (states - center_states).astype(jnp.bfloat16)
        analysed = jnp.einsum('jvbc,bjk->kvbc', anomalies.astype(jnp.float32), transform.astype(jnp.float32))
        analysed = (analysed + center_states).astype(jnp.bfloat16)
        return analysed.reshape(K, V, C_DEV)
    pieces = lax.map(one_column_group, jnp.arange(N_GRID, dtype=jnp.int32))
    return jnp.moveaxis(pieces, 0, 2).reshape(K, V, N_GRID * C_DEV)
```

```python
import jax
import jax.numpy as jnp
from jax import lax
from jax.experimental import pallas as pl
from jax.experimental.pallas import tpu as pltpu
from jax.sharding import PartitionSpec as P

MESH = pl.DeviceIdType.MESH
F32 = jnp.float32
BF16 = jnp.bfloat16

K = 80
KLOC = 10
V = 160
NM = 8
NG = 64
NY = 4
NZ = 16
ROWS = 2048
MLOC = 512
ENT = 2 * MLOC
CAP = 128
NQ = 8
REACH = 4
ITERS = 5
TV = 16
CHUNK = 2
NCHUNK = V // (TV * CHUNK)
PARTS = ((0, 3), (3, 3), (6, 4))
KCHIP = 2 * KLOC
TABLE = 96
HALF = K // 2
PACK = HALF + 8
FARTHEST_FIRST = (3, 4, 2, 5, 1, 6, 0, 7)

NT = (((1,), (1,)), ((), ()))


def neighbour(g, q):
    offset = q + 1 if q < REACH else q + NG - 2 * REACH
    return lax.rem(g + offset, NG)


def split(x):
    high = x.astype(BF16)
    return high, (x - high.astype(F32)).astype(BF16)


def mm(a, b):
    return jnp.dot(a, b, preferred_element_type=F32)


def mm_nt(a, b):
    return lax.dot_general(a, b, NT, preferred_element_type=F32)


def mm3(a, b):
    ah, al = split(a)
    bh, bl = split(b)
    return mm(ah, bh) + (mm(ah, bl) + mm(al, bh))


def body_kernel(
    ens_ref, prior_ref, value_ref, precision_ref, ids_ref, count_ref, taper_ref, out_ref,
    table, value_v, precision_v, ids_v, taper_v, count_s,
    listed_out, req_out, req_in, resp_out, resp_in, details_out, details_in, gram, gram_in,
    states, flat, result, anomalies, means, transforms, sending,
    ready, in_sem, own_sem, ens_send, ens_recv, relay_send, req_send, req_recv, resp_send, resp_recv,
    details_send, details_recv,
    gram_send, gram_recv, out_send, out_recv, out_own,
):
    m = lax.axis_index("mem")
    g = lax.axis_index("grid")
    y, core = m // 2, lax.rem(m, 2)
    z = lax.rem(g, NZ)

    def peer(p):
        return lax.rem(m + p, NM)

    def device(dy, c):
        return lax.rem(y + dy + NY, NY) * 2 + c

    def depth_of(q):
        return lax.rem(neighbour(g, q), NZ)

    barrier = pltpu.get_barrier_semaphore()
    for q in FARTHEST_FIRST:

        @pl.when(depth_of(q) > z)
        def _():
            pl.semaphore_signal(barrier, inc=1, device_id=(m, neighbour(g, q)), device_id_type=MESH)

    for p in (4, 2, 6, 3, 5, 1, 7):
        pl.semaphore_signal(barrier, inc=1, device_id=(peer(p), g), device_id_type=MESH)
    greetings = NM - 1
    for q in range(NQ):
        greetings = greetings + (depth_of(q) < z).astype(jnp.int32)

    loads = [
        pltpu.make_async_copy(ids_ref, ids_v, in_sem.at[0]),
        pltpu.make_async_copy(taper_ref, taper_v, in_sem.at[1]),
        pltpu.make_async_copy(count_ref, count_s, in_sem.at[2]),
        pltpu.make_async_copy(value_ref, value_v, in_sem.at[3]),
        pltpu.make_async_copy(precision_ref, precision_v, in_sem.at[4]),
        pltpu.make_async_copy(prior_ref, table.at[pl.ds(0, K)], in_sem.at[5]),
    ]
    for load in loads:
        load.start()

    def block_of(ref, c):
        return ref.at[:, :, pl.ds(pl.multiple_of(c * 128, 128), 128)]

    own_states = pltpu.make_async_copy(
        block_of(ens_ref, core), states.at[pl.ds(m * KLOC, KLOC)], own_sem.at[0]
    )
    own_states.start()

    def rows_in(i):
        first, count = PARTS[i]
        return pl.ds(first * TV, count * TV)

    def states_to(i, dy, c, slot):
        return pltpu.make_async_remote_copy(
            src_ref=block_of(ens_ref, c).at[:, rows_in(i)],
            dst_ref=states.at[pl.ds(m * KLOC, KLOC), rows_in(i)],
            send_sem=ens_send.at[i, dy + 1, c],
            recv_sem=ens_recv.at[i, slot],
            device_id=(device(dy, c), g),
            device_id_type=MESH,
        )

    def states_to_sibling():
        return pltpu.make_async_remote_copy(
            src_ref=block_of(ens_ref, 1 - core),
            dst_ref=states.at[pl.ds(m * KLOC, KLOC)],
            send_sem=ens_send.at[0, 1, 0],
            recv_sem=ens_recv.at[0, 4],
            device_id=(device(0, 1 - core), g),
            device_id_type=MESH,
        )

    def hand_on(i, c):
        dy = 1 - 2 * c
        rows = pl.ds(device(-dy, c) * KLOC, KLOC)
        return pltpu.make_async_remote_copy(
            src_ref=states.at[rows, rows_in(i)],
            dst_ref=states.at[rows, rows_in(i)],
            send_sem=relay_send.at[i, c],
            recv_sem=ens_recv.at[i, 5 + c],
            device_id=(device(dy, core), g),
            device_id_type=MESH,
        )

    def relay(i):
        for c, slot in ((0, 0), (1, 3)):
            states_to(i, 1, 0, slot).wait_recv()
            hand_on(i, c).start()

    pl.semaphore_wait(barrier, greetings)
    for q in range(NQ):

        @pl.when(depth_of(q) < z)
        def _():
            pl.semaphore_signal(
                ready.at[NQ - 1 - q], inc=1, device_id=(m, neighbour(g, q)), device_id_type=MESH
            )

    for i in range(len(PARTS)):
        for c in range(2):
            for dy, slot in ((1, 0), (-1, 2)):
                states_to(i, dy, c, slot + core).start()
        if i == 0:
            states_to_sibling().start()

    for load in loads[:3]:
        load.wait()

    ids = jnp.concatenate([ids_v[0, 0, 0:1, :], ids_v[0, 0, 1:2, :]], axis=1)
    taper = jnp.concatenate([taper_v[0, 0, 0:1, :], taper_v[0, 0, 1:2, :]], axis=1)
    lane = lax.broadcasted_iota(jnp.int32, (1, ENT), 1)
    limit = jnp.where(lane < MLOC, count_s[0, 0, 0], count_s[0, 0, 1] + MLOC)
    taper = jnp.where(lane < limit, taper, 0.0)
    offset = ((ids >> 11) - g + NG) & (NG - 1)
    row = ids & (ROWS - 1)
    high = (row >> 8).astype(F32)
    low = (row & 255).astype(F32)
    bucket = jnp.where(offset <= REACH, offset - 1, offset - (NG - 2 * REACH))
    mine = bucket < 0
    named = bucket == lax.broadcasted_iota(jnp.int32, (NQ, ENT), 0)
    named_f = jnp.where(named, 1.0, 0.0)
    before = jnp.where(
        lax.broadcasted_iota(jnp.int32, (128, 128), 0)
        < lax.broadcasted_iota(jnp.int32, (128, 128), 1), 1.0, 0.0,
    ).astype(BF16)
    chunks = [named_f[:, c * 128 : (c + 1) * 128] for c in range(ENT // 128)]
    prefix = mm(jnp.concatenate(chunks, axis=0).astype(BF16), before)
    base = jnp.zeros((NQ, 1), F32)
    ranks = []
    for c, chunk in enumerate(chunks):
        ranks.append(jnp.where(chunk > 0.0, prefix[c * NQ : (c + 1) * NQ] + base, -1.0))
        base = base + jnp.sum(chunk, axis=1, keepdims=True)
    rank = jnp.concatenate(ranks, axis=1)

    t1 = taper.astype(BF16).astype(F32)
    t2 = (taper - t1).astype(BF16).astype(F32)
    t3 = taper - t1 - t2
    kind = lax.broadcasted_iota(jnp.int32, (16, ENT), 0)
    entry = lax.broadcasted_iota(jnp.int32, (16, ENT), 1)
    first_block = entry < MLOC
    listed = jnp.where(kind == 0, high, jnp.where(kind == 1, low, 0.0))
    for b in range(2):
        for i, part in enumerate((t1, t2, t3)):
            here = (kind == 2 + 3 * b + i) & (first_block if b == 0 else ~first_block)
            listed = jnp.where(here, part, listed)
    listed = listed.astype(BF16)
    slot = lax.broadcasted_iota(jnp.int32, (CAP, 256), 0).astype(F32)
    for q in range(NQ):
        total = jnp.zeros((16, CAP), F32)
        for c in range(ENT // 256):
            cols = slice(c * 256, (c + 1) * 256)
            hit = jnp.where(slot == rank[q : q + 1, cols], 1.0, 0.0).astype(BF16)
            total = total + mm_nt(listed[:, cols], hit)
        listed_out[q] = total
        req_out[q] = total[0:2]

    def request(q, back):
        return pltpu.make_async_remote_copy(
            src_ref=req_out.at[q],
            dst_ref=req_in.at[back],
            send_sem=req_send.at[q],
            recv_sem=req_recv.at[back],
            device_id=(m, neighbour(g, q)),
            device_id_type=MESH,
        )

    for q in (3, 2, 1, 0, 7, 6, 5, 4):

        @pl.when(depth_of(q) > z)
        def _():
            pl.semaphore_wait(ready.at[q], 1)

        request(q, NQ - 1 - q).start()

    relay(0)

    for load in loads[3:]:
        load.wait()
    extra = lax.broadcasted_iota(jnp.int32, (TABLE - K, ROWS), 0)
    table[K:, :] = jnp.where(
        extra == 0, value_v[...].astype(F32).reshape(1, ROWS),
        jnp.where(extra == 1, precision_v[...].astype(F32).reshape(1, ROWS), 0.0),
    ).astype(BF16)

    depth = lax.broadcasted_iota(jnp.int32, (256, 256), 0).astype(F32)

    def columns_of(high, low):
        total = jnp.zeros((TABLE, 256), F32)
        for k in range(ROWS // 256):
            wanted = jnp.where(high == k, low, -1.0)
            hit = jnp.where(depth == wanted, 1.0, 0.0).astype(BF16)
            total = total + mm(table[:, k * 256 : (k + 1) * 256], hit)
        return total

    def response(q, back):
        return pltpu.make_async_remote_copy(
            src_ref=resp_out.at[q],
            dst_ref=resp_in.at[back],
            send_sem=resp_send.at[q],
            recv_sem=resp_recv.at[back],
            device_id=(m, neighbour(g, q)),
            device_id_type=MESH,
        )

    def details(q, back):
        return pltpu.make_async_remote_copy(
            src_ref=details_out.at[q],
            dst_ref=details_in.at[back],
            send_sem=details_send.at[q],
            recv_sem=details_recv.at[back],
            device_id=(m, neighbour(g, q)),
            device_id_type=MESH,
        )

    for q, r in ((0, 7), (1, 6), (2, 5), (3, 4)):
        request(q, q).wait_recv()
        request(r, r).wait_recv()
        asked = jnp.concatenate([req_in[q], req_in[r]], axis=1)
        found = columns_of(asked[0:1], asked[1:2])
        for i, side in ((q, slice(0, CAP)), (r, slice(CAP, 2 * CAP))):
            resp_out[i] = found[:K, side].astype(BF16)
            details_out[i] = found[K : K + 2, side]
            details(i, NQ - 1 - i).start()
            response(i, NQ - 1 - i).start()

    def gram_of(columns, value, precision, weights):
        center = jnp.sum(columns, axis=0, keepdims=True) * (1.0 / K)
        deviation = columns - center
        innovation = jnp.broadcast_to(value - center, (8, columns.shape[1]))
        nothing = jnp.zeros((K, columns.shape[1]), F32)
        top_h, top_l = split(jnp.concatenate([deviation, nothing[: 128 - K]], axis=0))
        low_h, low_l = split(jnp.concatenate([nothing, deviation[HALF:], nothing[:8]], axis=0))
        grams = []
        for weight in weights:
            weight = weight * precision
            upper_h, upper_l = split(jnp.concatenate([deviation[:HALF], innovation], axis=0) * weight)
            lower_h, lower_l = split(jnp.concatenate([deviation[HALF:] * weight, nothing[:8]], axis=0))
            grams.append(
                (mm_nt(upper_h, top_h) + mm_nt(lower_h, low_h))
                + (mm_nt(upper_h, top_l) + mm_nt(lower_h, low_l))
                + (mm_nt(upper_l, top_h) + mm_nt(lower_l, low_h))
            )
        return grams

    relay(1)
    own_taper = jnp.where(mine, taper, 0.0)
    for b in range(2):
        total = jnp.zeros((PACK, 128), F32)
        for c in range(2):
            cols = slice(b * MLOC + c * 256, b * MLOC + (c + 1) * 256)
            found = columns_of(high[:, cols], low[:, cols])
            total = total + gram_of(found[:K], found[K : K + 1], found[K + 1 : K + 2], (own_taper[:, cols],))[0]
        gram[b] = total

    for q, r in ((0, 7), (1, 6), (2, 5), (3, 4)):
        for i in (q, r):
            details(i, i).wait_recv()
            response(i, i).wait_recv()
        columns = jnp.concatenate([resp_in[q], resp_in[r]], axis=1).astype(F32)
        known = jnp.concatenate([details_in[q], details_in[r]], axis=1)
        asked = jnp.concatenate([listed_out[q], listed_out[r]], axis=1)
        weights = [asked[2 + 3 * b : 3 + 3 * b] + asked[3 + 3 * b : 4 + 3 * b] + asked[4 + 3 * b : 5 + 3 * b]
                   for b in range(2)]
        for b, part in enumerate(gram_of(columns, known[0:1], known[1:2], weights)):
            gram[b] = gram[b] + part

    def gram_to(p):
        target = peer(p)
        return pltpu.make_async_remote_copy(
            src_ref=gram.at[lax.rem(target, 2)],
            dst_ref=gram_in.at[p],
            send_sem=gram_send.at[p],
            recv_sem=gram_recv.at[p],
            device_id=(target, g),
            device_id_type=MESH,
        )

    for p in range(1, NM):
        gram_to(p).start()
    relay(2)

    own_states.wait()
    states_to_sibling().wait_recv()
    def prepare(t, carry):
        x = states[:, pl.ds(pl.multiple_of(t * TV, TV), TV), :].astype(F32)
        mean = jnp.sum(x, axis=0) * (1.0 / K)
        means[t] = mean
        flat[...] = (x - mean).reshape(K * TV, 128)
        for v in range(TV):
            anomalies[t, :, v * 128 : (v + 1) * 128] = flat[pl.ds(v, K, stride=TV), :].astype(BF16)
        return carry

    def complete(i):
        for slot in (1, 2):
            states_to(i, 1, 0, slot).wait_recv()
        for c in range(2):
            hand_on(i, c).wait_recv()
        first, count = PARTS[i]
        lax.fori_loop(first, first + count, prepare, 0)

    complete(0)
    complete(1)

    total = gram[core]
    for p in range(1, NM):
        gram_to(p).wait_recv()
        total = total + gram_in[p]

    same = (lax.broadcasted_iota(jnp.int32, (K, K), 0) == lax.broadcasted_iota(jnp.int32, (K, K), 1))
    identity = jnp.where(same, 1.0, 0.0)
    drive = total[HALF : HALF + 1, :K]
    turned = jnp.transpose(total)[HALF:K, :HALF]
    corner = total[:HALF, K : K + HALF]
    gram_total = jnp.concatenate([total[:HALF, :K], jnp.concatenate([turned, corner], axis=1)], axis=0)
    system = gram_total + (K - 1.0) * identity
    scale = jnp.sqrt(jnp.sum(system * system, axis=(0, 1), keepdims=True))
    root_iter = system * (1.0 / scale)
    inverse_root = 1.5 * identity - 0.5 * root_iter
    root_iter = mm3(root_iter, inverse_root)
    for step in range(1, ITERS):
        update = 1.5 * identity - 0.5 * mm3(inverse_root, root_iter)
        if step < ITERS - 1:
            root_iter = mm3(root_iter, update)
        inverse_root = mm3(update, inverse_root)
    shift = mm3(mm3(jnp.broadcast_to(drive, (8, K)), inverse_root), inverse_root)[0:1] / scale
    transforms[...] = jnp.sqrt((K - 1.0) / scale) * inverse_root + shift
    transform = transforms[pl.ds(y * KCHIP, KCHIP), :].astype(BF16)

    def rows_of(i):
        return pl.ds(pl.multiple_of(i * (CHUNK * TV), TV), CHUNK * TV)

    def result_to_sibling(i):
        return pltpu.make_async_remote_copy(
            src_ref=sending.at[pl.ds((1 - core) * KLOC, KLOC), rows_of(i)],
            dst_ref=block_of(out_ref, core).at[:, rows_of(i)],
            send_sem=out_send.at[i],
            recv_sem=out_recv.at[i],
            device_id=(device(0, 1 - core), g),
            device_id_type=MESH,
        )

    def result_own(i):
        return pltpu.make_async_copy(
            sending.at[pl.ds(core * KLOC, KLOC), rows_of(i)],
            block_of(out_ref, core).at[:, rows_of(i)],
            out_own.at[i],
        )

    def analyse(i, carry):
        for j in range(CHUNK):
            t = i * CHUNK + j
            mean = means[t]
            moved = mm(transform, anomalies[t])
            for v in range(TV):
                result[pl.ds(v, KCHIP, stride=TV), :] = moved[:, v * 128 : (v + 1) * 128] + mean[v : v + 1]
            sending[:, pl.ds(pl.multiple_of(t * TV, TV), TV), :] = (
                result[...].reshape(KCHIP, TV, 128).astype(BF16)
            )
        result_to_sibling(i).start()
        result_own(i).start()
        return carry

    lax.fori_loop(0, PARTS[2][0] // CHUNK, analyse, 0)
    complete(2)
    lax.fori_loop(PARTS[2][0] // CHUNK, NCHUNK, analyse, 0)

    for i in range(NCHUNK):
        result_to_sibling(i).wait_recv()
        result_to_sibling(i).wait_send()
        result_own(i).wait()
    for i in range(len(PARTS)):
        for c in range(2):
            for dy in (1, -1):
                states_to(i, dy, c, 0).wait_send()
            hand_on(i, c).wait_send()
    states_to_sibling().wait_send()
    for p in range(1, NM):
        gram_to(p).wait_send()

    for q in range(NQ):
        request(q, NQ - 1 - q).wait_send()
        response(q, NQ - 1 - q).wait_send()
        details(q, NQ - 1 - q).wait_send()


def body(ensemble, obs_prior, obs_value, obs_precision, entry_ids, entry_count, entry_taper):
    hbm = pl.BlockSpec(memory_space=pltpu.HBM)
    dma = pltpu.SemaphoreType.DMA
    return pl.pallas_call(
        body_kernel,
        out_shape=jax.ShapeDtypeStruct(ensemble.shape, ensemble.dtype),
        in_specs=[hbm] * 7,
        out_specs=hbm,
        scratch_shapes=[
            pltpu.VMEM((TABLE, ROWS), BF16),
            pltpu.VMEM((ROWS,), BF16),
            pltpu.VMEM((ROWS,), BF16),
            pltpu.VMEM((1, 1, 2, MLOC), jnp.int32),
            pltpu.VMEM((1, 1, 2, MLOC), F32),
            pltpu.SMEM((1, 1, 2), jnp.int32),
            pltpu.VMEM((NQ, 16, CAP), F32),
            pltpu.VMEM((NQ, 2, CAP), F32),
            pltpu.VMEM((NQ, 2, CAP), F32),
            pltpu.VMEM((NQ, K, CAP), BF16),
            pltpu.VMEM((NQ, K, CAP), BF16),
            pltpu.VMEM((NQ, 2, CAP), F32),
            pltpu.VMEM((NQ, 2, CAP), F32),
            pltpu.VMEM((2, PACK, 128), F32),
            pltpu.VMEM((NM, PACK, 128), F32),
            pltpu.VMEM((K, V, 128), BF16),
            pltpu.VMEM((K * TV, 128), F32),
            pltpu.VMEM((KCHIP * TV, 128), F32),
            pltpu.VMEM((V // TV, K, TV * 128), BF16),
            pltpu.VMEM((V // TV, TV, 128), F32),
            pltpu.VMEM((K, K), F32),
            pltpu.VMEM((KCHIP, V, 128), BF16),
            pltpu.SemaphoreType.REGULAR((NQ,)),
            dma((6,)),
            dma((1,)),
            dma((3, 3, 2)),
            dma((3, 7)),
            dma((3, 2)),
            dma((NQ,)),
            dma((NQ,)),
            dma((NQ,)),
            dma((NQ,)),
            dma((NQ,)),
            dma((NQ,)),
            dma((NM,)),
            dma((NM,)),
            dma((NCHUNK,)),
            dma((NCHUNK,)),
            dma((NCHUNK,)),
        ],
        compiler_params=pltpu.CompilerParams(
            collective_id=0, has_side_effects=True, vmem_limit_bytes=60 * 1024 * 1024
        ),
        name="analysis",
    )(ensemble, obs_prior, obs_value, obs_precision, entry_ids, entry_count, entry_taper)


def solution(mesh):
    return jax.shard_map(
        body,
        mesh=mesh,
        in_specs=(
            P("mem", None, "grid"),
            P(None, ("mem", "grid")),
            P(("mem", "grid")),
            P(("mem", "grid")),
            P("mem", "grid", None, None),
            P("mem", "grid", None),
            P("mem", "grid", None, None),
        ),
        out_specs=P("mem", None, "grid"),
        check_vma=False,
    )
```

```python
import jax
import jax.numpy as jnp
from jax import lax
from jax.experimental import pallas as pl
from jax.experimental.pallas import tpu as pltpu
from jax.sharding import PartitionSpec as P

MESH = pl.DeviceIdType.MESH
F32 = jnp.float32
BF16 = jnp.bfloat16

K = 80
KLOC = 10
V = 160
NM = 8
NG = 64
NY = 4
NZ = 16
ROWS = 2048
MLOC = 512
ENT = 2 * MLOC
CAP = 128
NQ = 8
REACH = 4
ITERS = 5
TV = 16
TILES = V // TV
PARTS = ((0, 3), (3, 3), (6, 4))
KCHIP = 2 * KLOC
TABLE = 96
HALF = K // 2
PACK = HALF + 8
FARTHEST_FIRST = (3, 4, 2, 5, 1, 6, 0, 7)

NT = (((1,), (1,)), ((), ()))


def neighbour(g, q):
    offset = q + 1 if q < REACH else q + NG - 2 * REACH
    return lax.rem(g + offset, NG)


def split(x):
    high = x.astype(BF16)
    return high, (x - high.astype(F32)).astype(BF16)


def mm(a, b):
    return jnp.dot(a, b, preferred_element_type=F32)


def mm_nt(a, b):
    return lax.dot_general(a, b, NT, preferred_element_type=F32)


def mm3(a, b):
    ah, al = split(a)
    bh, bl = split(b)
    halves = jnp.concatenate([bh, bl], axis=1)
    halves = jnp.concatenate([halves, jnp.zeros((128 - K, 256), BF16)], axis=0)
    rows = a.shape[0]
    parts = mm(jnp.concatenate([ah, al], axis=0), halves)
    return parts[:rows, :128] + (parts[:rows, 128:] + parts[rows:, :128])


def body_kernel(
    ens_ref, prior_ref, value_ref, precision_ref, ids_ref, count_ref, taper_ref, out_ref,
    table, value_v, precision_v, ids_v, taper_v, count_s,
    listed_out, req_out, req_in, resp_out, resp_in, details_out, details_in, gram, gram_in,
    states, result, anomalies, means, transforms, sending,
    ready, in_sem, own_sem, ens_send, ens_recv, relay_send, req_send, req_recv, resp_send, resp_recv,
    details_send, details_recv,
    gram_send, gram_recv, out_send, out_recv, out_own,
):
    m = lax.axis_index("mem")
    g = lax.axis_index("grid")
    y, core = m // 2, lax.rem(m, 2)
    z = lax.rem(g, NZ)

    def peer(p):
        return lax.rem(m + p, NM)

    def device(dy, c):
        return lax.rem(y + dy + NY, NY) * 2 + c

    def depth_of(q):
        return lax.rem(neighbour(g, q), NZ)

    barrier = pltpu.get_barrier_semaphore()
    for q in FARTHEST_FIRST:

        @pl.when(depth_of(q) > z)
        def _():
            pl.semaphore_signal(barrier, inc=1, device_id=(m, neighbour(g, q)), device_id_type=MESH)

    for p in (4, 2, 6, 3, 5, 1, 7):
        pl.semaphore_signal(barrier, inc=1, device_id=(peer(p), g), device_id_type=MESH)
    greetings = NM - 1
    for q in range(NQ):
        greetings = greetings + (depth_of(q) < z).astype(jnp.int32)

    loads = [
        pltpu.make_async_copy(ids_ref, ids_v, in_sem.at[0]),
        pltpu.make_async_copy(taper_ref, taper_v, in_sem.at[1]),
        pltpu.make_async_copy(count_ref, count_s, in_sem.at[2]),
        pltpu.make_async_copy(value_ref, value_v, in_sem.at[3]),
        pltpu.make_async_copy(precision_ref, precision_v, in_sem.at[4]),
        pltpu.make_async_copy(prior_ref, table.at[pl.ds(0, K)], in_sem.at[5]),
    ]
    for load in loads:
        load.start()

    def block_of(ref, c):
        return ref.at[:, :, pl.ds(pl.multiple_of(c * 128, 128), 128)]

    own_states = pltpu.make_async_copy(
        block_of(ens_ref, core), states.at[pl.ds(m * KLOC, KLOC)], own_sem.at[0]
    )
    own_states.start()

    def rows_in(i):
        first, count = PARTS[i]
        return pl.ds(first * TV, count * TV)

    def states_to(i, dy, c, slot):
        return pltpu.make_async_remote_copy(
            src_ref=block_of(ens_ref, c).at[:, rows_in(i)],
            dst_ref=states.at[pl.ds(m * KLOC, KLOC), rows_in(i)],
            send_sem=ens_send.at[i, dy + 1, c],
            recv_sem=ens_recv.at[i, slot],
            device_id=(device(dy, c), g),
            device_id_type=MESH,
        )

    def states_to_sibling():
        return pltpu.make_async_remote_copy(
            src_ref=block_of(ens_ref, 1 - core),
            dst_ref=states.at[pl.ds(m * KLOC, KLOC)],
            send_sem=ens_send.at[0, 1, 0],
            recv_sem=ens_recv.at[0, 4],
            device_id=(device(0, 1 - core), g),
            device_id_type=MESH,
        )

    def hand_on(i, c):
        dy = 1 - 2 * c
        rows = pl.ds(device(-dy, c) * KLOC, KLOC)
        return pltpu.make_async_remote_copy(
            src_ref=states.at[rows, rows_in(i)],
            dst_ref=states.at[rows, rows_in(i)],
            send_sem=relay_send.at[i, c],
            recv_sem=ens_recv.at[i, 5 + c],
            device_id=(device(dy, core), g),
            device_id_type=MESH,
        )

    def relay(i):
        for c, slot in ((0, 0), (1, 3)):
            states_to(i, 1, 0, slot).wait_recv()
            hand_on(i, c).start()

    pl.semaphore_wait(barrier, greetings)
    for q in FARTHEST_FIRST:

        @pl.when(depth_of(q) < z)
        def _():
            pl.semaphore_signal(
                ready.at[NQ - 1 - q], inc=1, device_id=(m, neighbour(g, q)), device_id_type=MESH
            )

    for i in range(len(PARTS)):
        for c in range(2):
            for dy, slot in ((1, 0), (-1, 2)):
                states_to(i, dy, c, slot + core).start()
        if i == 0:
            states_to_sibling().start()

    for load in loads[:3]:
        load.wait()

    ids = jnp.concatenate([ids_v[0, 0, 0:1, :], ids_v[0, 0, 1:2, :]], axis=1)
    taper = jnp.concatenate([taper_v[0, 0, 0:1, :], taper_v[0, 0, 1:2, :]], axis=1)
    lane = lax.broadcasted_iota(jnp.int32, (1, ENT), 1)
    limit = jnp.where(lane < MLOC, count_s[0, 0, 0], count_s[0, 0, 1] + MLOC)
    taper = jnp.where(lane < limit, taper, 0.0)
    offset = ((ids >> 11) - g + NG) & (NG - 1)
    row = ids & (ROWS - 1)
    high = (row >> 8).astype(F32)
    low = (row & 255).astype(F32)
    bucket = jnp.where(offset <= REACH, offset - 1, offset - (NG - 2 * REACH))
    mine = bucket < 0
    named = bucket == lax.broadcasted_iota(jnp.int32, (NQ, ENT), 0)
    named_f = jnp.where(named, 1.0, 0.0)
    before = jnp.where(
        lax.broadcasted_iota(jnp.int32, (128, 128), 0)
        < lax.broadcasted_iota(jnp.int32, (128, 128), 1), 1.0, 0.0,
    ).astype(BF16)
    chunks = [named_f[:, c * 128 : (c + 1) * 128] for c in range(ENT // 128)]
    prefix = mm(jnp.concatenate(chunks, axis=0).astype(BF16), before)
    base = jnp.zeros((NQ, 1), F32)
    ranks = []
    for c, chunk in enumerate(chunks):
        ranks.append(jnp.where(chunk > 0.0, prefix[c * NQ : (c + 1) * NQ] + base, -1.0))
        base = base + jnp.sum(chunk, axis=1, keepdims=True)
    rank = jnp.concatenate(ranks, axis=1)

    t1 = taper.astype(BF16).astype(F32)
    t2 = (taper - t1).astype(BF16).astype(F32)
    t3 = taper - t1 - t2
    kind = lax.broadcasted_iota(jnp.int32, (16, ENT), 0)
    entry = lax.broadcasted_iota(jnp.int32, (16, ENT), 1)
    first_block = entry < MLOC
    listed = jnp.where(kind == 0, high, jnp.where(kind == 1, low, 0.0))
    for b in range(2):
        for i, part in enumerate((t1, t2, t3)):
            here = (kind == 2 + 3 * b + i) & (first_block if b == 0 else ~first_block)
            listed = jnp.where(here, part, listed)
    listed = listed.astype(BF16)
    slot = lax.broadcasted_iota(jnp.int32, (CAP, 256), 0).astype(F32)
    for q in range(NQ):
        total = jnp.zeros((16, CAP), F32)
        for c in range(ENT // 256):
            cols = slice(c * 256, (c + 1) * 256)
            hit = jnp.where(slot == rank[q : q + 1, cols], 1.0, 0.0).astype(BF16)
            total = total + mm_nt(listed[:, cols], hit)
        listed_out[q] = total
        req_out[q] = total[0:2]

    def request(q, back):
        return pltpu.make_async_remote_copy(
            src_ref=req_out.at[q],
            dst_ref=req_in.at[back],
            send_sem=req_send.at[q],
            recv_sem=req_recv.at[back],
            device_id=(m, neighbour(g, q)),
            device_id_type=MESH,
        )

    for q in (3, 2, 1, 0, 7, 6, 5, 4):

        @pl.when(depth_of(q) > z)
        def _():
            pl.semaphore_wait(ready.at[q], 1)

        request(q, NQ - 1 - q).start()

    relay(0)

    for load in loads[3:]:
        load.wait()
    extra = lax.broadcasted_iota(jnp.int32, (TABLE - K, ROWS), 0)
    table[K:, :] = jnp.where(
        extra == 0, value_v[...].astype(F32).reshape(1, ROWS),
        jnp.where(extra == 1, precision_v[...].astype(F32).reshape(1, ROWS), 0.0),
    ).astype(BF16)

    depth = lax.broadcasted_iota(jnp.int32, (256, 256), 0).astype(F32)

    def columns_of(high, low):
        total = jnp.zeros((TABLE, 256), F32)
        for k in range(ROWS // 256):
            wanted = jnp.where(high == k, low, -1.0)
            hit = jnp.where(depth == wanted, 1.0, 0.0).astype(BF16)
            total = total + mm(table[:, k * 256 : (k + 1) * 256], hit)
        return total

    def response(q, back):
        return pltpu.make_async_remote_copy(
            src_ref=resp_out.at[q],
            dst_ref=resp_in.at[back],
            send_sem=resp_send.at[q],
            recv_sem=resp_recv.at[back],
            device_id=(m, neighbour(g, q)),
            device_id_type=MESH,
        )

    def details(q, back):
        return pltpu.make_async_remote_copy(
            src_ref=details_out.at[q],
            dst_ref=details_in.at[back],
            send_sem=details_send.at[q],
            recv_sem=details_recv.at[back],
            device_id=(m, neighbour(g, q)),
            device_id_type=MESH,
        )

    for q, r in ((0, 7), (1, 6), (2, 5), (3, 4)):
        request(q, q).wait_recv()
        request(r, r).wait_recv()
        asked = jnp.concatenate([req_in[q], req_in[r]], axis=1)
        found = columns_of(asked[0:1], asked[1:2])
        for i, side in ((q, slice(0, CAP)), (r, slice(CAP, 2 * CAP))):
            resp_out[i] = found[:K, side].astype(BF16)
            details_out[i] = found[K : K + 2, side]
            details(i, NQ - 1 - i).start()
            response(i, NQ - 1 - i).start()

    def gram_of(columns, value, precision, weights):
        center = jnp.sum(columns, axis=0, keepdims=True) * (1.0 / K)
        deviation = columns - center
        innovation = jnp.broadcast_to(value - center, (8, columns.shape[1]))
        nothing = jnp.zeros((K, columns.shape[1]), F32)
        top_h, top_l = split(jnp.concatenate([deviation, nothing[: 128 - K]], axis=0))
        low_h, low_l = split(jnp.concatenate([nothing, deviation[HALF:], nothing[:8]], axis=0))
        grams = []
        for weight in weights:
            weight = weight * precision
            upper_h, upper_l = split(jnp.concatenate([deviation[:HALF], innovation], axis=0) * weight)
            lower_h, lower_l = split(jnp.concatenate([deviation[HALF:] * weight, nothing[:8]], axis=0))
            grams.append(
                (mm_nt(upper_h, top_h) + mm_nt(lower_h, low_h))
                + (mm_nt(upper_h, top_l) + mm_nt(lower_h, low_l))
                + (mm_nt(upper_l, top_h) + mm_nt(lower_l, low_h))
            )
        return grams

    relay(1)
    own_taper = jnp.where(mine, taper, 0.0)
    for b in range(2):
        total = jnp.zeros((PACK, 128), F32)
        for c in range(2):
            cols = slice(b * MLOC + c * 256, b * MLOC + (c + 1) * 256)
            found = columns_of(high[:, cols], low[:, cols])
            total = total + gram_of(found[:K], found[K : K + 1], found[K + 1 : K + 2], (own_taper[:, cols],))[0]
        gram[b] = total

    for q, r in ((0, 7), (1, 6), (2, 5), (3, 4)):
        for i in (q, r):
            details(i, i).wait_recv()
            response(i, i).wait_recv()
        columns = jnp.concatenate([resp_in[q], resp_in[r]], axis=1).astype(F32)
        known = jnp.concatenate([details_in[q], details_in[r]], axis=1)
        asked = jnp.concatenate([listed_out[q], listed_out[r]], axis=1)
        weights = [asked[2 + 3 * b : 3 + 3 * b] + asked[3 + 3 * b : 4 + 3 * b] + asked[4 + 3 * b : 5 + 3 * b]
                   for b in range(2)]
        for b, part in enumerate(gram_of(columns, known[0:1], known[1:2], weights)):
            gram[b] = gram[b] + part

    def gram_to(p):
        target = peer(p)
        return pltpu.make_async_remote_copy(
            src_ref=gram.at[lax.rem(target, 2)],
            dst_ref=gram_in.at[p],
            send_sem=gram_send.at[p],
            recv_sem=gram_recv.at[p],
            device_id=(target, g),
            device_id_type=MESH,
        )

    for p in (4, 3, 5, 2, 6, 1, 7):
        gram_to(p).start()
    relay(2)

    own_states.wait()
    states_to_sibling().wait_recv()
    def prepare(t, carry):
        x = states[:, pl.ds(pl.multiple_of(t * TV, TV), TV), :].astype(F32)
        mean = jnp.sum(x, axis=0) * (1.0 / K)
        means[t] = mean
        turned = jnp.swapaxes(x - mean, 0, 1)
        for v in range(TV):
            anomalies[t, :, v * 128 : (v + 1) * 128] = turned[v].astype(BF16)
        return carry

    def complete(i):
        for slot in (1, 2):
            states_to(i, 1, 0, slot).wait_recv()
        for c in range(2):
            hand_on(i, c).wait_recv()
        first, count = PARTS[i]
        lax.fori_loop(first, first + count, prepare, 0)

    complete(0)
    complete(1)

    total = gram[core]
    for p in range(1, NM):
        gram_to(p).wait_recv()
        total = total + gram_in[p]

    same = lax.broadcasted_iota(jnp.int32, (K, 128), 0) == lax.broadcasted_iota(jnp.int32, (K, 128), 1)
    identity = jnp.where(same, 1.0, 0.0)
    drive = total[HALF : HALF + 1]
    turned = jnp.transpose(total)[HALF:K, :HALF]
    corner = total[:HALF, K : K + HALF]
    lower = jnp.concatenate([turned, corner, jnp.zeros((HALF, 128 - K), F32)], axis=1)
    inside = lax.broadcasted_iota(jnp.int32, (HALF, 128), 1) < K
    upper = jnp.where(inside, total[:HALF], 0.0)
    system = jnp.concatenate([upper, lower], axis=0) + (K - 1.0) * identity
    scale = jnp.sqrt(jnp.sum(system * system, axis=(0, 1), keepdims=True))
    root_iter = system * (1.0 / scale)
    inverse_root = 1.5 * identity - 0.5 * root_iter
    root_iter = mm3(root_iter, inverse_root)
    for step in range(1, ITERS):
        update = 1.5 * identity - 0.5 * mm3(inverse_root, root_iter)
        if step < ITERS - 1:
            root_iter = mm3(root_iter, update)
        inverse_root = mm3(update, inverse_root)
    shift = mm3(mm3(jnp.broadcast_to(drive, (16, 128)), inverse_root), inverse_root)[0:1] / scale
    transforms[...] = jnp.sqrt((K - 1.0) / scale) * inverse_root + shift
    transform = transforms[pl.ds(y * KCHIP, KCHIP), :][:, :K].astype(BF16)

    def rows_of(i):
        return pl.ds(pl.multiple_of(i * TV, TV), TV)

    def result_to_sibling(i):
        return pltpu.make_async_remote_copy(
            src_ref=sending.at[pl.ds((1 - core) * KLOC, KLOC), rows_of(i)],
            dst_ref=block_of(out_ref, core).at[:, rows_of(i)],
            send_sem=out_send.at[i],
            recv_sem=out_recv.at[i],
            device_id=(device(0, 1 - core), g),
            device_id_type=MESH,
        )

    def result_own(i):
        return pltpu.make_async_copy(
            sending.at[pl.ds(core * KLOC, KLOC), rows_of(i)],
            block_of(out_ref, core).at[:, rows_of(i)],
            out_own.at[i],
        )

    def analyse(t, carry):
        moved = mm(transform, anomalies[t])
        mean = means[t]
        for v in range(TV):
            result[pl.ds(v, KCHIP, stride=TV), :] = moved[:, v * 128 : (v + 1) * 128] + mean[v : v + 1]
        sending[:, rows_of(t), :] = result[...].reshape(KCHIP, TV, 128).astype(BF16)
        result_to_sibling(t).start()
        result_own(t).start()
        return carry

    late = PARTS[2][0]
    lax.fori_loop(0, late, analyse, 0)
    complete(2)
    lax.fori_loop(late, TILES, analyse, 0)

    for i in range(TILES):
        result_to_sibling(i).wait_recv()
        result_to_sibling(i).wait_send()
        result_own(i).wait()
    for i in range(len(PARTS)):
        for c in range(2):
            for dy in (1, -1):
                states_to(i, dy, c, 0).wait_send()
            hand_on(i, c).wait_send()
    states_to_sibling().wait_send()
    for p in range(1, NM):
        gram_to(p).wait_send()

    for q in range(NQ):
        request(q, NQ - 1 - q).wait_send()
        response(q, NQ - 1 - q).wait_send()
        details(q, NQ - 1 - q).wait_send()


def body(ensemble, obs_prior, obs_value, obs_precision, entry_ids, entry_count, entry_taper):
    hbm = pl.BlockSpec(memory_space=pltpu.HBM)
    dma = pltpu.SemaphoreType.DMA
    return pl.pallas_call(
        body_kernel,
        out_shape=pltpu.VMEM(ensemble.shape, ensemble.dtype),
        in_specs=[hbm] * 7,
        out_specs=pl.BlockSpec(memory_space=pltpu.VMEM),
        scratch_shapes=[
            pltpu.VMEM((TABLE, ROWS), BF16),
            pltpu.VMEM((ROWS,), BF16),
            pltpu.VMEM((ROWS,), BF16),
            pltpu.VMEM((1, 1, 2, MLOC), jnp.int32),
            pltpu.VMEM((1, 1, 2, MLOC), F32),
            pltpu.SMEM((1, 1, 2), jnp.int32),
            pltpu.VMEM((NQ, 16, CAP), F32),
            pltpu.VMEM((NQ, 2, CAP), F32),
            pltpu.VMEM((NQ, 2, CAP), F32),
            pltpu.VMEM((NQ, K, CAP), BF16),
            pltpu.VMEM((NQ, K, CAP), BF16),
            pltpu.VMEM((NQ, 2, CAP), F32),
            pltpu.VMEM((NQ, 2, CAP), F32),
            pltpu.VMEM((2, PACK, 128), F32),
            pltpu.VMEM((NM, PACK, 128), F32),
            pltpu.VMEM((K, V, 128), BF16),
            pltpu.VMEM((KCHIP * TV, 128), F32),
            pltpu.VMEM((V // TV, K, TV * 128), BF16),
            pltpu.VMEM((V // TV, TV, 128), F32),
            pltpu.VMEM((K, 128), F32),
            pltpu.VMEM((KCHIP, V, 128), BF16),
            pltpu.SemaphoreType.REGULAR((NQ,)),
            dma((6,)),
            dma((1,)),
            dma((3, 3, 2)),
            dma((3, 7)),
            dma((3, 2)),
            dma((NQ,)),
            dma((NQ,)),
            dma((NQ,)),
            dma((NQ,)),
            dma((NQ,)),
            dma((NQ,)),
            dma((NM,)),
            dma((NM,)),
            dma((TILES,)),
            dma((TILES,)),
            dma((TILES,)),
        ],
        compiler_params=pltpu.CompilerParams(
            collective_id=0, has_side_effects=True, vmem_limit_bytes=60 * 1024 * 1024
        ),
        name="analysis",
    )(ensemble, obs_prior, obs_value, obs_precision, entry_ids, entry_count, entry_taper)


def solution(mesh):
    return jax.shard_map(
        body,
        mesh=mesh,
        in_specs=(
            P("mem", None, "grid"),
            P(None, ("mem", "grid")),
            P(("mem", "grid")),
            P(("mem", "grid")),
            P("mem", "grid", None, None),
            P("mem", "grid", None),
            P("mem", "grid", None, None),
        ),
        out_specs=P("mem", None, "grid"),
        check_vma=False,
    )
```

```python
import jax
import jax.numpy as jnp
from jax import lax
from jax.experimental import pallas as pl
from jax.experimental.pallas import tpu as pltpu
from jax.sharding import PartitionSpec as P

MESH = pl.DeviceIdType.MESH
F32 = jnp.float32
BF16 = jnp.bfloat16

K = 80
KLOC = 10
V = 160
NM = 8
NG = 64
NY = 4
NZ = 16
ROWS = 2048
MLOC = 512
ENT = 2 * MLOC
CAP = 128
NQ = 8
REACH = 4
ITERS = 5
TV = 16
TILES = V // TV
PARTS = ((0, 3), (3, 3), (6, 4))
KCHIP = 2 * KLOC
TABLE = 96
HALF = K // 2
PACK = HALF + 8
FARTHEST_FIRST = (3, 4, 2, 5, 1, 6, 0, 7)

NT = (((1,), (1,)), ((), ()))


def neighbour(g, q):
    offset = q + 1 if q < REACH else q + NG - 2 * REACH
    return lax.rem(g + offset, NG)


def split(x):
    high = x.astype(BF16)
    return high, (x - high.astype(F32)).astype(BF16)


def mm(a, b):
    return jnp.dot(a, b, preferred_element_type=F32)


def mm_nt(a, b):
    return lax.dot_general(a, b, NT, preferred_element_type=F32)


def mm3(a, b):
    ah, al = split(a)
    bh, bl = split(b)
    halves = jnp.concatenate([bh, bl], axis=1)
    halves = jnp.concatenate([halves, jnp.zeros((128 - K, 256), BF16)], axis=0)
    rows = a.shape[0]
    parts = mm(jnp.concatenate([ah, al], axis=0), halves)
    return parts[:rows, :128] + (parts[:rows, 128:] + parts[rows:, :128])


def body_kernel(
    ens_ref, prior_ref, value_ref, precision_ref, ids_ref, count_ref, taper_ref, out_ref,
    table, value_v, precision_v, ids_v, taper_v, count_s,
    listed_out, req_out, req_in, resp_out, resp_in, details_out, details_in, gram, gram_in,
    states, result, anomalies, means, transforms, sending,
    ready, in_sem, own_sem, ens_send, ens_recv, relay_send, req_send, req_recv, resp_send, resp_recv,
    details_send, details_recv,
    gram_send, gram_recv, out_send, out_recv, out_own,
):
    m = lax.axis_index("mem")
    g = lax.axis_index("grid")
    y, core = m // 2, lax.rem(m, 2)
    z = lax.rem(g, NZ)

    def peer(p):
        return lax.rem(m + p, NM)

    def device(dy, c):
        return lax.rem(y + dy + NY, NY) * 2 + c

    def depth_of(q):
        return lax.rem(neighbour(g, q), NZ)

    barrier = pltpu.get_barrier_semaphore()
    for q in FARTHEST_FIRST:

        @pl.when(depth_of(q) > z)
        def _():
            pl.semaphore_signal(barrier, inc=1, device_id=(m, neighbour(g, q)), device_id_type=MESH)

    for p in (4, 2, 6, 3, 5, 1, 7):
        pl.semaphore_signal(barrier, inc=1, device_id=(peer(p), g), device_id_type=MESH)
    greetings = NM - 1
    for q in range(NQ):
        greetings = greetings + (depth_of(q) < z).astype(jnp.int32)

    loads = [
        pltpu.make_async_copy(ids_ref, ids_v, in_sem.at[0]),
        pltpu.make_async_copy(taper_ref, taper_v, in_sem.at[1]),
        pltpu.make_async_copy(count_ref, count_s, in_sem.at[2]),
        pltpu.make_async_copy(value_ref, value_v, in_sem.at[3]),
        pltpu.make_async_copy(precision_ref, precision_v, in_sem.at[4]),
        pltpu.make_async_copy(prior_ref, table.at[pl.ds(0, K)], in_sem.at[5]),
    ]
    for load in loads:
        load.start()

    def block_of(ref, c):
        return ref.at[:, :, pl.ds(pl.multiple_of(c * 128, 128), 128)]

    own_states = pltpu.make_async_copy(
        block_of(ens_ref, core), states.at[pl.ds(m * KLOC, KLOC)], own_sem.at[0]
    )
    own_states.start()

    def rows_in(i):
        first, count = PARTS[i]
        return pl.ds(first * TV, count * TV)

    def states_to(i, dy, c, slot):
        return pltpu.make_async_remote_copy(
            src_ref=block_of(ens_ref, c).at[:, rows_in(i)],
            dst_ref=states.at[pl.ds(m * KLOC, KLOC), rows_in(i)],
            send_sem=ens_send.at[i, dy + 1, c],
            recv_sem=ens_recv.at[i, slot],
            device_id=(device(dy, c), g),
            device_id_type=MESH,
        )

    def states_to_sibling():
        return pltpu.make_async_remote_copy(
            src_ref=block_of(ens_ref, 1 - core),
            dst_ref=states.at[pl.ds(m * KLOC, KLOC)],
            send_sem=ens_send.at[0, 1, 0],
            recv_sem=ens_recv.at[0, 4],
            device_id=(device(0, 1 - core), g),
            device_id_type=MESH,
        )

    def hand_on(i, c):
        dy = 1 - 2 * c
        rows = pl.ds(device(-dy, c) * KLOC, KLOC)
        return pltpu.make_async_remote_copy(
            src_ref=states.at[rows, rows_in(i)],
            dst_ref=states.at[rows, rows_in(i)],
            send_sem=relay_send.at[i, c],
            recv_sem=ens_recv.at[i, 5 + c],
            device_id=(device(dy, core), g),
            device_id_type=MESH,
        )

    def relay(i):
        for c, slot in ((0, 0), (1, 3)):
            states_to(i, 1, 0, slot).wait_recv()
            hand_on(i, c).start()

    pl.semaphore_wait(barrier, greetings)
    for q in FARTHEST_FIRST:

        @pl.when(depth_of(q) < z)
        def _():
            pl.semaphore_signal(
                ready.at[NQ - 1 - q], inc=1, device_id=(m, neighbour(g, q)), device_id_type=MESH
            )

    for i in range(len(PARTS)):
        for c in range(2):
            for dy, slot in ((1, 0), (-1, 2)):
                states_to(i, dy, c, slot + core).start()
        if i == 0:
            states_to_sibling().start()

    for load in loads[:3]:
        load.wait()

    ids = jnp.concatenate([ids_v[0, 0, 0:1, :], ids_v[0, 0, 1:2, :]], axis=1)
    taper = jnp.concatenate([taper_v[0, 0, 0:1, :], taper_v[0, 0, 1:2, :]], axis=1)
    lane = lax.broadcasted_iota(jnp.int32, (1, ENT), 1)
    limit = jnp.where(lane < MLOC, count_s[0, 0, 0], count_s[0, 0, 1] + MLOC)
    taper = jnp.where(lane < limit, taper, 0.0)
    offset = ((ids >> 11) - g + NG) & (NG - 1)
    row = ids & (ROWS - 1)
    high = (row >> 8).astype(F32)
    low = (row & 255).astype(F32)
    bucket = jnp.where(offset <= REACH, offset - 1, offset - (NG - 2 * REACH))
    mine = bucket < 0
    named = bucket == lax.broadcasted_iota(jnp.int32, (NQ, ENT), 0)
    named_f = jnp.where(named, 1.0, 0.0)
    before = jnp.where(
        lax.broadcasted_iota(jnp.int32, (128, 128), 0)
        < lax.broadcasted_iota(jnp.int32, (128, 128), 1), 1.0, 0.0,
    ).astype(BF16)
    chunks = [named_f[:, c * 128 : (c + 1) * 128] for c in range(ENT // 128)]
    prefix = mm(jnp.concatenate(chunks, axis=0).astype(BF16), before)
    base = jnp.zeros((NQ, 1), F32)
    ranks = []
    for c, chunk in enumerate(chunks):
        ranks.append(jnp.where(chunk > 0.0, prefix[c * NQ : (c + 1) * NQ] + base, -1.0))
        base = base + jnp.sum(chunk, axis=1, keepdims=True)
    rank = jnp.concatenate(ranks, axis=1)

    t1 = taper.astype(BF16).astype(F32)
    t2 = (taper - t1).astype(BF16).astype(F32)
    t3 = taper - t1 - t2
    kind = lax.broadcasted_iota(jnp.int32, (16, ENT), 0)
    entry = lax.broadcasted_iota(jnp.int32, (16, ENT), 1)
    first_block = entry < MLOC
    listed = jnp.where(kind == 0, high, jnp.where(kind == 1, low, 0.0))
    for b in range(2):
        for i, part in enumerate((t1, t2, t3)):
            here = (kind == 2 + 3 * b + i) & (first_block if b == 0 else ~first_block)
            listed = jnp.where(here, part, listed)
    listed = listed.astype(BF16)
    slot = lax.broadcasted_iota(jnp.int32, (CAP, 256), 0).astype(F32)
    for q in range(NQ):
        total = jnp.zeros((16, CAP), F32)
        for c in range(ENT // 256):
            cols = slice(c * 256, (c + 1) * 256)
            hit = jnp.where(slot == rank[q : q + 1, cols], 1.0, 0.0).astype(BF16)
            total = total + mm_nt(listed[:, cols], hit)
        listed_out[q] = total
        req_out[q] = total[0:2]

    def request(q, back):
        return pltpu.make_async_remote_copy(
            src_ref=req_out.at[q],
            dst_ref=req_in.at[back],
            send_sem=req_send.at[q],
            recv_sem=req_recv.at[back],
            device_id=(m, neighbour(g, q)),
            device_id_type=MESH,
        )

    for q in (3, 2, 1, 0, 7, 6, 5, 4):

        @pl.when(depth_of(q) > z)
        def _():
            pl.semaphore_wait(ready.at[q], 1)

        request(q, NQ - 1 - q).start()

    for load in loads[3:]:
        load.wait()
    extra = lax.broadcasted_iota(jnp.int32, (TABLE - K, ROWS), 0)
    table[K:, :] = jnp.where(
        extra == 0, value_v[...].astype(F32).reshape(1, ROWS),
        jnp.where(extra == 1, precision_v[...].astype(F32).reshape(1, ROWS), 0.0),
    ).astype(BF16)

    depth = lax.broadcasted_iota(jnp.int32, (256, 256), 0).astype(F32)

    def columns_of(high, low):
        total = jnp.zeros((TABLE, 256), F32)
        for k in range(ROWS // 256):
            wanted = jnp.where(high == k, low, -1.0)
            hit = jnp.where(depth == wanted, 1.0, 0.0).astype(BF16)
            total = total + mm(table[:, k * 256 : (k + 1) * 256], hit)
        return total

    def response(q, back):
        return pltpu.make_async_remote_copy(
            src_ref=resp_out.at[q],
            dst_ref=resp_in.at[back],
            send_sem=resp_send.at[q],
            recv_sem=resp_recv.at[back],
            device_id=(m, neighbour(g, q)),
            device_id_type=MESH,
        )

    def details(q, back):
        return pltpu.make_async_remote_copy(
            src_ref=details_out.at[q],
            dst_ref=details_in.at[back],
            send_sem=details_send.at[q],
            recv_sem=details_recv.at[back],
            device_id=(m, neighbour(g, q)),
            device_id_type=MESH,
        )

    for q, r in ((0, 7), (1, 6), (2, 5), (3, 4)):
        request(q, q).wait_recv()
        request(r, r).wait_recv()
        asked = jnp.concatenate([req_in[q], req_in[r]], axis=1)
        found = columns_of(asked[0:1], asked[1:2])
        for i, side in ((q, slice(0, CAP)), (r, slice(CAP, 2 * CAP))):
            resp_out[i] = found[:K, side].astype(BF16)
            details_out[i] = found[K : K + 2, side]
            details(i, NQ - 1 - i).start()
            response(i, NQ - 1 - i).start()

    def gram_of(columns, value, precision, weights):
        center = jnp.sum(columns, axis=0, keepdims=True) * (1.0 / K)
        deviation = columns - center
        innovation = jnp.broadcast_to(value - center, (8, columns.shape[1]))
        nothing = jnp.zeros((K, columns.shape[1]), F32)
        top_h, top_l = split(jnp.concatenate([deviation, nothing[: 128 - K]], axis=0))
        low_h, low_l = split(jnp.concatenate([nothing, deviation[HALF:], nothing[:8]], axis=0))
        grams = []
        for weight in weights:
            weight = weight * precision
            upper_h, upper_l = split(jnp.concatenate([deviation[:HALF], innovation], axis=0) * weight)
            lower_h, lower_l = split(jnp.concatenate([deviation[HALF:] * weight, nothing[:8]], axis=0))
            grams.append(
                (mm_nt(upper_h, top_h) + mm_nt(lower_h, low_h))
                + (mm_nt(upper_h, top_l) + mm_nt(lower_h, low_l))
                + (mm_nt(upper_l, top_h) + mm_nt(lower_l, low_h))
            )
        return grams

    relay(0)
    relay(1)
    own_taper = jnp.where(mine, taper, 0.0)
    for b in range(2):
        total = jnp.zeros((PACK, 128), F32)
        for c in range(2):
            cols = slice(b * MLOC + c * 256, b * MLOC + (c + 1) * 256)
            found = columns_of(high[:, cols], low[:, cols])
            total = total + gram_of(found[:K], found[K : K + 1], found[K + 1 : K + 2], (own_taper[:, cols],))[0]
        gram[b] = total

    for q, r in ((0, 7), (1, 6), (2, 5), (3, 4)):
        for i in (q, r):
            details(i, i).wait_recv()
            response(i, i).wait_recv()
        columns = jnp.concatenate([resp_in[q], resp_in[r]], axis=1).astype(F32)
        known = jnp.concatenate([details_in[q], details_in[r]], axis=1)
        asked = jnp.concatenate([listed_out[q], listed_out[r]], axis=1)
        weights = [asked[2 + 3 * b : 3 + 3 * b] + asked[3 + 3 * b : 4 + 3 * b] + asked[4 + 3 * b : 5 + 3 * b]
                   for b in range(2)]
        for b, part in enumerate(gram_of(columns, known[0:1], known[1:2], weights)):
            gram[b] = gram[b] + part

    def gram_to(p):
        target = peer(p)
        return pltpu.make_async_remote_copy(
            src_ref=gram.at[lax.rem(target, 2)],
            dst_ref=gram_in.at[p],
            send_sem=gram_send.at[p],
            recv_sem=gram_recv.at[p],
            device_id=(target, g),
            device_id_type=MESH,
        )

    for p in (4, 3, 5, 2, 6, 1, 7):
        gram_to(p).start()
    relay(2)

    own_states.wait()
    states_to_sibling().wait_recv()
    def prepare(t, carry):
        x = states[:, pl.ds(pl.multiple_of(t * TV, TV), TV), :].astype(F32)
        mean = jnp.sum(x, axis=0) * (1.0 / K)
        means[t] = mean
        turned = jnp.swapaxes(x - mean, 0, 1)
        for v in range(TV):
            anomalies[t, :, v * 128 : (v + 1) * 128] = turned[v].astype(BF16)
        return carry

    def complete(i):
        for slot in (1, 2):
            states_to(i, 1, 0, slot).wait_recv()
        for c in range(2):
            hand_on(i, c).wait_recv()
        first, count = PARTS[i]
        step = 2 if count % 2 == 0 else 1

        def several(k, carry):
            for j in range(step):
                prepare(first + step * k + j, carry)
            return carry

        lax.fori_loop(0, count // step, several, 0)

    complete(0)
    complete(1)

    total = gram[core]
    for p in range(1, NM):
        gram_to(p).wait_recv()
        total = total + gram_in[p]

    same = lax.broadcasted_iota(jnp.int32, (K, 128), 0) == lax.broadcasted_iota(jnp.int32, (K, 128), 1)
    identity = jnp.where(same, 1.0, 0.0)
    drive = total[HALF : HALF + 1]
    turned = jnp.transpose(total)[HALF:K, :HALF]
    corner = total[:HALF, K : K + HALF]
    lower = jnp.concatenate([turned, corner, jnp.zeros((HALF, 128 - K), F32)], axis=1)
    inside = lax.broadcasted_iota(jnp.int32, (HALF, 128), 1) < K
    upper = jnp.where(inside, total[:HALF], 0.0)
    system = jnp.concatenate([upper, lower], axis=0) + (K - 1.0) * identity
    scale = jnp.sqrt(jnp.sum(system * system, axis=(0, 1), keepdims=True))
    root_iter = system * (1.0 / scale)
    inverse_root = 1.5 * identity - 0.5 * root_iter
    root_iter = mm3(root_iter, inverse_root)
    for step in range(1, ITERS):
        update = 1.5 * identity - 0.5 * mm3(inverse_root, root_iter)
        if step < ITERS - 1:
            root_iter = mm3(root_iter, update)
        inverse_root = mm3(update, inverse_root)
    shift = mm3(mm3(jnp.broadcast_to(drive, (16, 128)), inverse_root), inverse_root)[0:1] / scale
    transforms[:K] = jnp.sqrt((K - 1.0) / scale) * inverse_root + shift
    transform = transforms[pl.ds(y * KCHIP, KCHIP), :][:, :K].astype(BF16)

    def rows_of(i):
        return pl.ds(pl.multiple_of(i * TV, TV), TV)

    def result_to_sibling(i):
        return pltpu.make_async_remote_copy(
            src_ref=sending.at[pl.ds((1 - core) * KLOC, KLOC), rows_of(i)],
            dst_ref=block_of(out_ref, core).at[:, rows_of(i)],
            send_sem=out_send.at[i],
            recv_sem=out_recv.at[i],
            device_id=(device(0, 1 - core), g),
            device_id_type=MESH,
        )

    def result_own(i):
        return pltpu.make_async_copy(
            sending.at[pl.ds(core * KLOC, KLOC), rows_of(i)],
            block_of(out_ref, core).at[:, rows_of(i)],
            out_own.at[i],
        )

    def analyse(first, count):
        for j in range(count):
            t = first + j
            moved = mm(transform, anomalies[t])
            mean = means[t]
            for v in range(TV):
                result[j, pl.ds(v, KCHIP, stride=TV), :] = moved[:, v * 128 : (v + 1) * 128] + mean[v : v + 1]
        for j in range(count):
            t = first + j
            sending[:, t * TV : (t + 1) * TV, :] = result[j, : KCHIP * TV].reshape(KCHIP, TV, 128).astype(BF16)
            result_to_sibling(t).start()
            result_own(t).start()

    late = PARTS[2][0]
    analyse(0, 3)
    analyse(3, 3)
    complete(2)
    analyse(6, 4)

    for i in range(TILES):
        result_to_sibling(i).wait_recv()
        result_to_sibling(i).wait_send()
        result_own(i).wait()
    for i in range(len(PARTS)):
        for c in range(2):
            for dy in (1, -1):
                states_to(i, dy, c, 0).wait_send()
            hand_on(i, c).wait_send()
    states_to_sibling().wait_send()
    for p in range(1, NM):
        gram_to(p).wait_send()

    for q in range(NQ):
        request(q, NQ - 1 - q).wait_send()
        response(q, NQ - 1 - q).wait_send()
        details(q, NQ - 1 - q).wait_send()


def body(ensemble, obs_prior, obs_value, obs_precision, entry_ids, entry_count, entry_taper):
    hbm = pl.BlockSpec(memory_space=pltpu.HBM)
    dma = pltpu.SemaphoreType.DMA
    return pl.pallas_call(
        body_kernel,
        out_shape=pltpu.VMEM(ensemble.shape, ensemble.dtype),
        in_specs=[hbm] * 7,
        out_specs=pl.BlockSpec(memory_space=pltpu.VMEM),
        scratch_shapes=[
            pltpu.VMEM((TABLE, ROWS), BF16),
            pltpu.VMEM((ROWS,), BF16),
            pltpu.VMEM((ROWS,), BF16),
            pltpu.VMEM((1, 1, 2, MLOC), jnp.int32),
            pltpu.VMEM((1, 1, 2, MLOC), F32),
            pltpu.SMEM((1, 1, 2), jnp.int32),
            pltpu.VMEM((NQ, 16, CAP), F32),
            pltpu.VMEM((NQ + 4, 2, CAP), F32),
            pltpu.VMEM((NQ, 2, CAP), F32),
            pltpu.VMEM((NQ, K, CAP), BF16),
            pltpu.VMEM((NQ, K, CAP), BF16),
            pltpu.VMEM((NQ + 4, 2, CAP), F32),
            pltpu.VMEM((NQ, 2, CAP), F32),
            pltpu.VMEM((2, PACK, 128), F32),
            pltpu.VMEM((NM, PACK, 128), F32),
            pltpu.VMEM((K, V, 128), BF16),
            pltpu.VMEM((4, 24 * TV, 128), F32),
            pltpu.VMEM((V // TV, K, TV * 128), BF16),
            pltpu.VMEM((V // TV, TV, 128), F32),
            pltpu.VMEM((K + 8, 128), F32),
            pltpu.VMEM((KCHIP, V, 128), BF16),
            pltpu.SemaphoreType.REGULAR((NQ,)),
            dma((6,)),
            dma((1,)),
            dma((3, 3, 2)),
            dma((3, 7)),
            dma((3, 2)),
            dma((NQ,)),
            dma((NQ,)),
            dma((NQ,)),
            dma((NQ,)),
            dma((NQ,)),
            dma((NQ,)),
            dma((NM,)),
            dma((NM,)),
            dma((TILES,)),
            dma((TILES,)),
            dma((TILES,)),
        ],
        compiler_params=pltpu.CompilerParams(
            collective_id=0, has_side_effects=True, vmem_limit_bytes=60 * 1024 * 1024
        ),
        name="analysis",
    )(ensemble, obs_prior, obs_value, obs_precision, entry_ids, entry_count, entry_taper)


def solution(mesh):
    return jax.shard_map(
        body,
        mesh=mesh,
        in_specs=(
            P("mem", None, "grid"),
            P(None, ("mem", "grid")),
            P(("mem", "grid")),
            P(("mem", "grid")),
            P("mem", "grid", None, None),
            P("mem", "grid", None),
            P("mem", "grid", None, None),
        ),
        out_specs=P("mem", None, "grid"),
        check_vma=False,
    )
```

```python
import jax
import jax.numpy as jnp
from jax import lax
from jax.experimental import pallas as pl
from jax.experimental.pallas import tpu as pltpu
from jax.sharding import PartitionSpec as P

MESH = pl.DeviceIdType.MESH
F32 = jnp.float32
BF16 = jnp.bfloat16

K = 80
KLOC = 10
V = 160
NM = 8
NG = 64
NY = 4
NZ = 16
ROWS = 2048
MLOC = 512
ENT = 2 * MLOC
CAP = 128
NQ = 8
REACH = 4
ITERS = 5
TV = 16
TILES = V // TV
PARTS = ((0, 3), (3, 3), (6, 4))
KCHIP = 2 * KLOC
TABLE = 96
HALF = K // 2
PACK = HALF + 8
FARTHEST_FIRST = (3, 4, 2, 5, 1, 6, 0, 7)

NT = (((1,), (1,)), ((), ()))


def neighbour(g, q):
    offset = q + 1 if q < REACH else q + NG - 2 * REACH
    return lax.rem(g + offset, NG)


def split(x):
    high = x.astype(BF16)
    return high, (x - high.astype(F32)).astype(BF16)


def mm(a, b):
    return jnp.dot(a, b, preferred_element_type=F32)


def mm_nt(a, b):
    return lax.dot_general(a, b, NT, preferred_element_type=F32)


def mm3(a, b):
    ah, al = split(a)
    bh, bl = split(b)
    halves = jnp.concatenate([bh, bl], axis=1)
    halves = jnp.concatenate([halves, jnp.zeros((128 - K, 256), BF16)], axis=0)
    rows = a.shape[0]
    parts = mm(jnp.concatenate([ah, al], axis=0), halves)
    return parts[:rows, :128] + (parts[:rows, 128:] + parts[rows:, :128])


def body_kernel(
    ens_ref, prior_ref, value_ref, precision_ref, ids_ref, count_ref, taper_ref, out_ref,
    table, value_v, precision_v, ids_v, taper_v, count_s,
    listed_out, req_out, req_in, resp_out, resp_in, details_out, details_in, gram, gram_in,
    states, result, anomalies, means, transforms, sending,
    ready, in_sem, own_sem, ens_send, ens_recv, relay_send, req_send, req_recv, resp_send, resp_recv,
    details_send, details_recv,
    gram_send, gram_recv, out_send, out_recv, out_own,
):
    m = lax.axis_index("mem")
    g = lax.axis_index("grid")
    y, core = m // 2, lax.rem(m, 2)
    z = lax.rem(g, NZ)

    def peer(p):
        return lax.rem(m + p, NM)

    def device(dy, c):
        return lax.rem(y + dy + NY, NY) * 2 + c

    def depth_of(q):
        return lax.rem(neighbour(g, q), NZ)

    barrier = pltpu.get_barrier_semaphore()
    for q in FARTHEST_FIRST:

        @pl.when(depth_of(q) > z)
        def _():
            pl.semaphore_signal(barrier, inc=1, device_id=(m, neighbour(g, q)), device_id_type=MESH)

    for p in (4, 2, 6, 3, 5, 1, 7):
        pl.semaphore_signal(barrier, inc=1, device_id=(peer(p), g), device_id_type=MESH)
    greetings = NM - 1
    for q in range(NQ):
        greetings = greetings + (depth_of(q) < z).astype(jnp.int32)

    loads = [
        pltpu.make_async_copy(ids_ref, ids_v, in_sem.at[0]),
        pltpu.make_async_copy(taper_ref, taper_v, in_sem.at[1]),
        pltpu.make_async_copy(count_ref, count_s, in_sem.at[2]),
        pltpu.make_async_copy(value_ref, value_v, in_sem.at[3]),
        pltpu.make_async_copy(precision_ref, precision_v, in_sem.at[4]),
        pltpu.make_async_copy(prior_ref, table.at[pl.ds(0, K)], in_sem.at[5]),
    ]
    for load in loads:
        load.start()

    def block_of(ref, c):
        return ref.at[:, :, pl.ds(pl.multiple_of(c * 128, 128), 128)]

    own_states = pltpu.make_async_copy(
        block_of(ens_ref, core), states.at[pl.ds(m * KLOC, KLOC)], own_sem.at[0]
    )
    own_states.start()

    def rows_in(i):
        first, count = PARTS[i]
        return pl.ds(first * TV, count * TV)

    def states_to(i, dy, c, slot):
        return pltpu.make_async_remote_copy(
            src_ref=block_of(ens_ref, c).at[:, rows_in(i)],
            dst_ref=states.at[pl.ds(m * KLOC, KLOC), rows_in(i)],
            send_sem=ens_send.at[i, dy + 1, c],
            recv_sem=ens_recv.at[i, slot],
            device_id=(device(dy, c), g),
            device_id_type=MESH,
        )

    def states_to_sibling():
        return pltpu.make_async_remote_copy(
            src_ref=block_of(ens_ref, 1 - core),
            dst_ref=states.at[pl.ds(m * KLOC, KLOC)],
            send_sem=ens_send.at[0, 1, 0],
            recv_sem=ens_recv.at[0, 4],
            device_id=(device(0, 1 - core), g),
            device_id_type=MESH,
        )

    def hand_on(i, c):
        dy = 1 - 2 * c
        rows = pl.ds(device(-dy, c) * KLOC, KLOC)
        return pltpu.make_async_remote_copy(
            src_ref=states.at[rows, rows_in(i)],
            dst_ref=states.at[rows, rows_in(i)],
            send_sem=relay_send.at[i, c],
            recv_sem=ens_recv.at[i, 5 + c],
            device_id=(device(dy, core), g),
            device_id_type=MESH,
        )

    def relay(i):
        for c, slot in ((0, 0), (1, 3)):
            states_to(i, 1, 0, slot).wait_recv()
            hand_on(i, c).start()

    pl.semaphore_wait(barrier, greetings)
    for q in FARTHEST_FIRST:

        @pl.when(depth_of(q) < z)
        def _():
            pl.semaphore_signal(
                ready.at[NQ - 1 - q], inc=1, device_id=(m, neighbour(g, q)), device_id_type=MESH
            )

    for i in range(len(PARTS)):
        for c in range(2):
            for dy, slot in ((1, 0), (-1, 2)):
                states_to(i, dy, c, slot + core).start()
        if i == 0:
            states_to_sibling().start()

    for load in loads[:3]:
        load.wait()

    ids = jnp.concatenate([ids_v[0, 0, 0:1, :], ids_v[0, 0, 1:2, :]], axis=1)
    taper = jnp.concatenate([taper_v[0, 0, 0:1, :], taper_v[0, 0, 1:2, :]], axis=1)
    lane = lax.broadcasted_iota(jnp.int32, (1, ENT), 1)
    limit = jnp.where(lane < MLOC, count_s[0, 0, 0], count_s[0, 0, 1] + MLOC)
    taper = jnp.where(lane < limit, taper, 0.0)
    offset = ((ids >> 11) - g + NG) & (NG - 1)
    row = ids & (ROWS - 1)
    high = (row >> 8).astype(F32)
    low = (row & 255).astype(F32)
    bucket = jnp.where(offset <= REACH, offset - 1, offset - (NG - 2 * REACH))
    mine = bucket < 0
    named = bucket == lax.broadcasted_iota(jnp.int32, (NQ, ENT), 0)
    named_f = jnp.where(named, 1.0, 0.0)
    before = jnp.where(
        lax.broadcasted_iota(jnp.int32, (128, 128), 0)
        < lax.broadcasted_iota(jnp.int32, (128, 128), 1), 1.0, 0.0,
    ).astype(BF16)
    chunks = [named_f[:, c * 128 : (c + 1) * 128] for c in range(ENT // 128)]
    prefix = mm(jnp.concatenate(chunks, axis=0).astype(BF16), before)
    base = jnp.zeros((NQ, 1), F32)
    ranks = []
    for c, chunk in enumerate(chunks):
        ranks.append(jnp.where(chunk > 0.0, prefix[c * NQ : (c + 1) * NQ] + base, -1.0))
        base = base + jnp.sum(chunk, axis=1, keepdims=True)
    rank = jnp.concatenate(ranks, axis=1)

    t1 = taper.astype(BF16).astype(F32)
    t2 = (taper - t1).astype(BF16).astype(F32)
    t3 = taper - t1 - t2
    kind = lax.broadcasted_iota(jnp.int32, (16, ENT), 0)
    entry = lax.broadcasted_iota(jnp.int32, (16, ENT), 1)
    first_block = entry < MLOC
    listed = jnp.where(kind == 0, high, jnp.where(kind == 1, low, 0.0))
    for b in range(2):
        for i, part in enumerate((t1, t2, t3)):
            here = (kind == 2 + 3 * b + i) & (first_block if b == 0 else ~first_block)
            listed = jnp.where(here, part, listed)
    listed = listed.astype(BF16)
    slot = lax.broadcasted_iota(jnp.int32, (CAP, 256), 0).astype(F32)
    for q in range(NQ):
        total = jnp.zeros((16, CAP), F32)
        for c in range(ENT // 256):
            cols = slice(c * 256, (c + 1) * 256)
            hit = jnp.where(slot == rank[q : q + 1, cols], 1.0, 0.0).astype(BF16)
            total = total + mm_nt(listed[:, cols], hit)
        listed_out[q] = total
        req_out[q] = total[0:2]

    def request(q, back):
        return pltpu.make_async_remote_copy(
            src_ref=req_out.at[q],
            dst_ref=req_in.at[back],
            send_sem=req_send.at[q],
            recv_sem=req_recv.at[back],
            device_id=(m, neighbour(g, q)),
            device_id_type=MESH,
        )

    for q in (3, 2, 1, 0, 7, 6, 5, 4):

        @pl.when(depth_of(q) > z)
        def _():
            pl.semaphore_wait(ready.at[q], 1)

        request(q, NQ - 1 - q).start()

    for load in loads[3:]:
        load.wait()
    extra = lax.broadcasted_iota(jnp.int32, (TABLE - K, ROWS), 0)
    table[K:, :] = jnp.where(
        extra == 0, value_v[...].astype(F32).reshape(1, ROWS),
        jnp.where(extra == 1, precision_v[...].astype(F32).reshape(1, ROWS), 0.0),
    ).astype(BF16)

    depth = lax.broadcasted_iota(jnp.int32, (256, 256), 0).astype(F32)

    def columns_of(high, low):
        total = jnp.zeros((TABLE, 256), F32)
        for k in range(ROWS // 256):
            wanted = jnp.where(high == k, low, -1.0)
            hit = jnp.where(depth == wanted, 1.0, 0.0).astype(BF16)
            total = total + mm(table[:, k * 256 : (k + 1) * 256], hit)
        return total

    def response(q, back):
        return pltpu.make_async_remote_copy(
            src_ref=resp_out.at[q],
            dst_ref=resp_in.at[back],
            send_sem=resp_send.at[q],
            recv_sem=resp_recv.at[back],
            device_id=(m, neighbour(g, q)),
            device_id_type=MESH,
        )

    def details(q, back):
        return pltpu.make_async_remote_copy(
            src_ref=details_out.at[q],
            dst_ref=details_in.at[back],
            send_sem=details_send.at[q],
            recv_sem=details_recv.at[back],
            device_id=(m, neighbour(g, q)),
            device_id_type=MESH,
        )

    for q, r in ((0, 7), (1, 6), (2, 5), (3, 4)):
        request(q, q).wait_recv()
        request(r, r).wait_recv()
        asked = jnp.concatenate([req_in[q], req_in[r]], axis=1)
        found = columns_of(asked[0:1], asked[1:2])
        for i, side in ((q, slice(0, CAP)), (r, slice(CAP, 2 * CAP))):
            resp_out[i] = found[:K, side].astype(BF16)
            details_out[i] = found[K : K + 2, side]
            details(i, NQ - 1 - i).start()
            response(i, NQ - 1 - i).start()

    def gram_of(columns, value, precision, weights):
        center = jnp.sum(columns, axis=0, keepdims=True) * (1.0 / K)
        deviation = columns - center
        innovation = jnp.broadcast_to(value - center, (8, columns.shape[1]))
        nothing = jnp.zeros((K, columns.shape[1]), F32)
        top_h, top_l = split(jnp.concatenate([deviation, nothing[: 128 - K]], axis=0))
        low_h, low_l = split(jnp.concatenate([nothing, deviation[HALF:], nothing[:8]], axis=0))
        grams = []
        for weight in weights:
            weight = weight * precision
            upper_h, upper_l = split(jnp.concatenate([deviation[:HALF], innovation], axis=0) * weight)
            lower_h, lower_l = split(jnp.concatenate([deviation[HALF:] * weight, nothing[:8]], axis=0))
            grams.append(
                (mm_nt(upper_h, top_h) + mm_nt(lower_h, low_h))
                + (mm_nt(upper_h, top_l) + mm_nt(lower_h, low_l))
                + (mm_nt(upper_l, top_h) + mm_nt(lower_l, low_h))
            )
        return grams

    relay(0)
    relay(1)
    own_taper = jnp.where(mine, taper, 0.0)
    for b in range(2):
        total = jnp.zeros((PACK, 128), F32)
        for c in range(2):
            cols = slice(b * MLOC + c * 256, b * MLOC + (c + 1) * 256)
            found = columns_of(high[:, cols], low[:, cols])
            total = total + gram_of(found[:K], found[K : K + 1], found[K + 1 : K + 2], (own_taper[:, cols],))[0]
        gram[b] = total

    for q, r in ((0, 7), (1, 6), (2, 5), (3, 4)):
        for i in (q, r):
            details(i, i).wait_recv()
            response(i, i).wait_recv()
        columns = jnp.concatenate([resp_in[q], resp_in[r]], axis=1).astype(F32)
        known = jnp.concatenate([details_in[q], details_in[r]], axis=1)
        asked = jnp.concatenate([listed_out[q], listed_out[r]], axis=1)
        weights = [asked[2 + 3 * b : 3 + 3 * b] + asked[3 + 3 * b : 4 + 3 * b] + asked[4 + 3 * b : 5 + 3 * b]
                   for b in range(2)]
        for b, part in enumerate(gram_of(columns, known[0:1], known[1:2], weights)):
            gram[b] = gram[b] + part

    def gram_to(p):
        target = peer(p)
        return pltpu.make_async_remote_copy(
            src_ref=gram.at[lax.rem(target, 2)],
            dst_ref=gram_in.at[p],
            send_sem=gram_send.at[p],
            recv_sem=gram_recv.at[p],
            device_id=(target, g),
            device_id_type=MESH,
        )

    for p in (4, 3, 5, 2, 6, 1, 7):
        gram_to(p).start()
    relay(2)

    own_states.wait()
    states_to_sibling().wait_recv()
    def prepare(t, carry):
        x = states[:, pl.ds(pl.multiple_of(t * TV, TV), TV), :].astype(F32)
        mean = jnp.sum(x, axis=0) * (1.0 / K)
        means[t] = mean
        turned = jnp.swapaxes(x - mean, 0, 1)
        for v in range(TV):
            anomalies[t, :, v * 128 : (v + 1) * 128] = turned[v].astype(BF16)
        return carry

    def complete(i):
        for slot in (1, 2):
            states_to(i, 1, 0, slot).wait_recv()
        for c in range(2):
            hand_on(i, c).wait_recv()
        first, count = PARTS[i]
        step = 2 if count % 2 == 0 else 1

        def several(k, carry):
            for j in range(step):
                prepare(first + step * k + j, carry)
            return carry

        lax.fori_loop(0, count // step, several, 0)

    complete(0)
    complete(1)

    total = gram[core]
    for p in range(1, NM):
        gram_to(p).wait_recv()
        total = total + gram_in[p]

    same = lax.broadcasted_iota(jnp.int32, (K, 128), 0) == lax.broadcasted_iota(jnp.int32, (K, 128), 1)
    identity = jnp.where(same, 1.0, 0.0)
    drive = total[HALF : HALF + 1]
    turned = jnp.transpose(total)[HALF:K, :HALF]
    corner = total[:HALF, K : K + HALF]
    lower = jnp.concatenate([turned, corner, jnp.zeros((HALF, 128 - K), F32)], axis=1)
    inside = lax.broadcasted_iota(jnp.int32, (HALF, 128), 1) < K
    upper = jnp.where(inside, total[:HALF], 0.0)
    system = jnp.concatenate([upper, lower], axis=0) + (K - 1.0) * identity
    scale = jnp.sqrt(jnp.sum(system * system, axis=(0, 1), keepdims=True))
    root_iter = system * (1.0 / scale)
    inverse_root = 1.5 * identity - 0.5 * root_iter
    root_iter = mm3(root_iter, inverse_root)
    for step in range(1, ITERS):
        update = 1.5 * identity - 0.5 * mm3(inverse_root, root_iter)
        if step < ITERS - 1:
            root_iter = mm3(root_iter, update)
        inverse_root = mm3(update, inverse_root)
    shift = mm3(mm3(jnp.broadcast_to(drive, (16, 128)), inverse_root), inverse_root)[0:1] / scale
    transforms[:K] = jnp.sqrt((K - 1.0) / scale) * inverse_root + shift
    transform = transforms[pl.ds(y * KCHIP, KCHIP), :][:, :K].astype(BF16)

    def rows_of(i):
        return pl.ds(pl.multiple_of(i * TV, TV), TV)

    def result_to_sibling(i):
        return pltpu.make_async_remote_copy(
            src_ref=sending.at[pl.ds((1 - core) * KLOC, KLOC), rows_of(i)],
            dst_ref=block_of(out_ref, core).at[:, rows_of(i)],
            send_sem=out_send.at[i],
            recv_sem=out_recv.at[i],
            device_id=(device(0, 1 - core), g),
            device_id_type=MESH,
        )

    def result_own(i):
        return pltpu.make_async_copy(
            sending.at[pl.ds(core * KLOC, KLOC), rows_of(i)],
            block_of(out_ref, core).at[:, rows_of(i)],
            out_own.at[i],
        )

    def analyse(first, count):
        for j in range(count):
            t = first + j
            moved = mm(transform, anomalies[t])
            mean = means[t]
            for v in range(TV):
                result[j, pl.ds(v, KCHIP, stride=TV), :] = moved[:, v * 128 : (v + 1) * 128] + mean[v : v + 1]
        for j in range(count):
            t = first + j
            sending[:, t * TV : (t + 1) * TV, :] = result[j, : KCHIP * TV].reshape(KCHIP, TV, 128).astype(BF16)
            result_to_sibling(t).start()
            result_own(t).start()

    late = PARTS[2][0]
    analyse(0, 3)
    analyse(3, 3)
    complete(2)
    analyse(6, 2)
    analyse(8, 2)

    for i in range(TILES):
        result_to_sibling(i).wait_recv()
        result_to_sibling(i).wait_send()
        result_own(i).wait()
    for i in range(len(PARTS)):
        for c in range(2):
            for dy in (1, -1):
                states_to(i, dy, c, 0).wait_send()
            hand_on(i, c).wait_send()
    states_to_sibling().wait_send()
    for p in range(1, NM):
        gram_to(p).wait_send()

    for q in range(NQ):
        request(q, NQ - 1 - q).wait_send()
        response(q, NQ - 1 - q).wait_send()
        details(q, NQ - 1 - q).wait_send()


def body(ensemble, obs_prior, obs_value, obs_precision, entry_ids, entry_count, entry_taper):
    hbm = pl.BlockSpec(memory_space=pltpu.HBM)
    dma = pltpu.SemaphoreType.DMA
    return pl.pallas_call(
        body_kernel,
        out_shape=pltpu.VMEM(ensemble.shape, ensemble.dtype),
        in_specs=[hbm] * 7,
        out_specs=pl.BlockSpec(memory_space=pltpu.VMEM),
        scratch_shapes=[
            pltpu.VMEM((TABLE, ROWS), BF16),
            pltpu.VMEM((ROWS,), BF16),
            pltpu.VMEM((ROWS,), BF16),
            pltpu.VMEM((1, 1, 2, MLOC), jnp.int32),
            pltpu.VMEM((1, 1, 2, MLOC), F32),
            pltpu.SMEM((1, 1, 2), jnp.int32),
            pltpu.VMEM((NQ, 16, CAP), F32),
            pltpu.VMEM((NQ + 4, 2, CAP), F32),
            pltpu.VMEM((NQ, 2, CAP), F32),
            pltpu.VMEM((NQ, K, CAP), BF16),
            pltpu.VMEM((NQ, K, CAP), BF16),
            pltpu.VMEM((NQ + 4, 2, CAP), F32),
            pltpu.VMEM((NQ, 2, CAP), F32),
            pltpu.VMEM((2, PACK, 128), F32),
            pltpu.VMEM((NM, PACK, 128), F32),
            pltpu.VMEM((K, V, 128), BF16),
            pltpu.VMEM((4, 24 * TV, 128), F32),
            pltpu.VMEM((V // TV, K, TV * 128), BF16),
            pltpu.VMEM((V // TV, TV, 128), F32),
            pltpu.VMEM((K + 8, 128), F32),
            pltpu.VMEM((KCHIP, V, 128), BF16),
            pltpu.SemaphoreType.REGULAR((NQ,)),
            dma((6,)),
            dma((1,)),
            dma((3, 3, 2)),
            dma((3, 7)),
            dma((3, 2)),
            dma((NQ,)),
            dma((NQ,)),
            dma((NQ,)),
            dma((NQ,)),
            dma((NQ,)),
            dma((NQ,)),
            dma((NM,)),
            dma((NM,)),
            dma((TILES,)),
            dma((TILES,)),
            dma((TILES,)),
        ],
        compiler_params=pltpu.CompilerParams(
            collective_id=0, has_side_effects=True, vmem_limit_bytes=60 * 1024 * 1024
        ),
        name="analysis",
    )(ensemble, obs_prior, obs_value, obs_precision, entry_ids, entry_count, entry_taper)


def solution(mesh):
    return jax.shard_map(
        body,
        mesh=mesh,
        in_specs=(
            P("mem", None, "grid"),
            P(None, ("mem", "grid")),
            P(("mem", "grid")),
            P(("mem", "grid")),
            P("mem", "grid", None, None),
            P("mem", "grid", None),
            P("mem", "grid", None, None),
        ),
        out_specs=P("mem", None, "grid"),
        check_vma=False,
    )
```
